256 devices in a mesh: ctx: 16 (over y, x), head: 8 (over z), batch: 2 (over core).
Axes of the slice: x: 4, y: 4, z: 8, core: 2. Of those that a mesh axis runs over, the one named last changes fastest.
Arguments:
- queries: bfloat16 [4096, 16384], P(('batch', 'ctx'), 'head'), parts along dimension 0, may hold values from -6 to 6
- new_keys: bfloat16 [4096, 1024], P(('batch', 'ctx'), 'head'), parts along dimension 0, may hold values from -6 to 6
- new_values: bfloat16 [4096, 1024], P(('batch', 'ctx'), 'head'), parts along dimension 0, may hold values from -6 to 6
- cache_keys: bfloat16 [16384, 1024], P(('batch', 'ctx'), 'head'), parts along dimension 0, may hold values from -6 to 6
- cache_values: bfloat16 [16384, 1024], P(('batch', 'ctx'), 'head'), parts along dimension 0, may hold values from -6 to 6
- cache_lens: int32 [32], P('batch'), parts along dimension 0, may hold values from 1 to 512, 5120 in all
- new_pos: int32 [4096], P('batch'), parts along dimension 0, may hold values from 0 to 2047, each once
Outputs:
- attended: bfloat16 [4096, 16384], P(('batch', 'ctx'), 'head'), parts along dimension 0
The draws below stay inside these ranges and needn't reach their ends.
There are 2 independent parts, one for each index of `batch`. The reference program is written for one: setup_inputs(seed, part) draws one part's arguments, and reference() takes and returns one part's arrays. A program takes and returns all parts, laid end to end along the dimension named above; each array names one. Nothing has to cross between parts.
Inputs may be any that keep to these rules, and one draw needn't show every extreme that they name: `cache_lens`: every block holds at least one filled slot, and in every request some block is full with 512. `new_pos`: each position appears once.
All inputs are finite; a program needn't handle non-finite values.
Results may differ from the reference program's by a relative error of at most 0.0055.
Values may be sent and summed in bfloat16 or wider, within the bound.
No kernel may reach another device: no remote copies, remote signals or barrier semaphores. Data moves between devices by JAX's collectives and lax.ppermute only.
A program may use at most 128 MiB of HBM per device.

```python
import math
import jax
import jax.numpy as jnp
import numpy as np
from jax import lax

HQ = 128
KVH = 8
HD = 128
TOK_DEV = 128
C_DEV = 512
NEW = 2048
CACHE = 8192
N_CTX = 16


def draw_queries(key, part):
    key = jax.random.fold_in(key, 1)
    base = jnp.clip(1.75 * jax.random.normal(key, (NEW, HQ * HD), jnp.float32), -6.0, 6.0)
    return base.astype(jnp.bfloat16)


def draw_cache_keys(key, part):
    key = jax.random.fold_in(key, 2)
    base = jnp.clip(1.75 * jax.random.normal(key, (CACHE, KVH * HD), jnp.float32), -6.0, 6.0)
    return base.astype(jnp.bfloat16)


def shard_levels(own_key, dims, shards, low, largest):
    gain = 1.0
    for dim, shards_of in shards:
        draws = jax.random.uniform(jax.random.fold_in(jax.random.fold_in(own_key, 6), dim), (shards_of,), jnp.float32, low / len(shards), largest / len(shards))
        gain = gain * jnp.repeat(jnp.exp(draws), dims[dim] // shards_of).reshape((-1,) + (1,) * (len(dims) - 1 - dim))
    return gain


def profile(count, total, limit, skew):
    portions = [(1 << 20) // math.isqrt(standing ** skew) + 1 for standing in range(2, count + 1)]
    spare, given = total - limit - (count - 1), [1] * (count - 1)
    while spare > 0:
        candidates = [i for i in range(count - 1) if given[i] < limit]
        pool, left = sum([portions[i] for i in candidates]), spare
        for i in candidates:
            addition = min(limit - given[i], max(1, left * portions[i] // pool), spare)
            given[i] = given[i] + addition
            spare = spare - addition
    return np.array([limit] + given)


def ragged(stream_key, amount, total, limit, slope):
    if amount == 2:
        one = jax.random.randint(stream_key, (), max(1, total - limit), min(limit, total - 1) + 1)
        return jnp.stack([one, total - one])
    tallies = jnp.asarray(profile(amount, total, limit, slope), jnp.int32)
    twos = (amount - 1) // 2
    source_of, taker = tallies[1:1 + 2 * twos:2], tallies[2:2 + 2 * twos:2]
    margin = jnp.minimum(source_of - 1, limit - taker)
    shifted = jax.random.randint(jax.random.fold_in(stream_key, 1), (twos,), 0, 1 << 20) % (margin + 1)
    tallies = tallies.at[1:1 + 2 * twos:2].set(source_of - shifted).at[2:2 + 2 * twos:2].set(taker + shifted)
    return tallies[jax.random.permutation(jax.random.fold_in(stream_key, 2), amount)]


def centred(stream_key, dims, width, most, split=(), kind=jnp.bfloat16):
    loudness = shard_levels(stream_key, dims, split, -0.22, 0.18) if split else 1.0
    values = jax.random.normal(stream_key, dims, jnp.float32) * width * loudness
    return jnp.minimum(jnp.maximum(values, -most), most).astype(kind)


def setup_inputs(seed: int = 0, part: int = 0) -> dict:
    seeds = jax.random.split(jax.random.key(seed), 8)
    part_keys = jax.random.split(jax.random.fold_in(seeds[7], part), 8)
    queries = draw_queries(jax.random.fold_in(jax.random.fold_in(seeds[7], part), 71), part)
    new_keys = centred(part_keys[1], (NEW, KVH * HD), 1.75, 6.0, ((0, 16), (1, 8)))
    new_values = centred(part_keys[2], (NEW, KVH * HD), 1.0, 6.0, ((0, 16), (1, 8)))
    cache_keys = draw_cache_keys(jax.random.fold_in(jax.random.fold_in(seeds[7], part), 71), part)
    cache_values = centred(part_keys[4], (CACHE, KVH * HD), 1.0, 6.0, ((0, 16), (1, 8)))
    cache_lens = ragged(part_keys[5], N_CTX, (5 * C_DEV * N_CTX) // 8, C_DEV, 2).astype(jnp.int32)
    new_pos = jax.random.permutation(part_keys[6], NEW).astype(jnp.int32)
    return dict(queries=queries, new_keys=new_keys, new_values=new_values, cache_keys=cache_keys, cache_values=cache_values, cache_lens=cache_lens, new_pos=new_pos)


NEG = -1e30


def reference(queries, new_keys, new_values, cache_keys, cache_values, cache_lens, new_pos):
    group = HQ // KVH
    scale = HD ** -0.5
    query = jnp.moveaxis(queries.reshape(NEW, KVH, group, HD), 1, 0)
    fresh_keys = new_keys.reshape(N_CTX, TOK_DEV, KVH, HD)
    fresh_values = new_values.reshape(N_CTX, TOK_DEV, KVH, HD)
    stored_keys = cache_keys.reshape(N_CTX, C_DEV, KVH, HD)
    stored_values = cache_values.reshape(N_CTX, C_DEV, KVH, HD)
    key_pos = new_pos.reshape(N_CTX, TOK_DEV)

    def one_block(carry, inputs):
        top, total, accum = carry
        kept_keys, kept_values, block_keys, block_values, length, block_pos = inputs
        keys = jnp.moveaxis(jnp.concatenate([kept_keys, block_keys], 0), 1, 0)
        values = jnp.moveaxis(jnp.concatenate([kept_values, block_values], 0), 1, 0)
        filled = jnp.arange(C_DEV, dtype=jnp.int32) < length
        visible = jnp.concatenate([jnp.broadcast_to(filled[None, :], (NEW, C_DEV)),
                                   block_pos[None, :] <= new_pos[:, None]], 1)

        def one_group(items):
            query_g, keys_g, values_g = items
            scores = jnp.einsum("nrd,kd->nrk", query_g.astype(jnp.float32), keys_g.astype(jnp.float32)) * scale
            scores = jnp.where(visible[:, None, :], scores, NEG)
            peak = scores.max(-1)
            weights = jnp.where(visible[:, None, :], jnp.exp(scores - peak[..., None]), 0.0)
            summed = weights.sum(-1)
            rounded = lax.optimization_barrier(weights.astype(jnp.bfloat16)).astype(jnp.float32)
            accum_g = jnp.einsum("nrk,kd->nrd", rounded, values_g.astype(jnp.float32))
            return accum_g / summed[..., None], peak + jnp.log(summed)

        partial_value, lse = lax.map(one_group, (query, keys, values))
        newest = jnp.maximum(top, lse)
        factor = jnp.exp(top - newest)
        weight = jnp.exp(lse - newest)
        return (newest, factor * total + weight, factor[..., None] * accum + weight[..., None] * partial_value), None

    start = (jnp.full((KVH, NEW, group), NEG, jnp.float32), jnp.zeros((KVH, NEW, group), jnp.float32),
             jnp.zeros((KVH, NEW, group, HD), jnp.float32))
    (top, total, accum), unused = lax.scan(one_block, start, (stored_keys, stored_values, fresh_keys, fresh_values,
                                                              cache_lens, key_pos))
    merged = accum / total[..., None]
    return jnp.moveaxis(merged, 0, 1).reshape(NEW, HQ * HD).astype(jnp.bfloat16)
```

```python
import functools
import jax
import jax.numpy as jnp
from jax import lax
from jax.experimental import pallas as pl
from jax.experimental.pallas import tpu as pltpu
from jax.sharding import PartitionSpec as P

HD = 128
SIDE = 4
HG = 4
NEG = -1e30
LIMIT = 1e37
VMEM = 40 * 2**20
LOG2E = 1.4426950408889634

OWN = ((0, 0),)
NEAR = ((0, -1), (0, 1), (-1, 0), (1, 0))
FAR = ((0, 2), (2, 0))
DIAG = ((-1, -1), (1, -1), (-1, 1), (1, 1))
REST = ((2, -1), (2, 1), (-1, 2), (1, 2), (2, 2))
ORDER = OWN + NEAR + FAR + DIAG + REST


def from_offset(block, dy, dx):
    route = []
    for y in range(SIDE):
        for x in range(SIDE):
            route.append((((y + dy) % SIDE) * SIDE + (x + dx) % SIDE, y * SIDE + x))
    return lax.ppermute(block, "ctx", route)


def rows_of(q_ref):
    return jnp.concatenate([q_ref[:, i * HD:(i + 1) * HD] for i in range(HG)], 0)


def own_columns(pos_ref, me, tokens):
    row = pos_ref[pl.ds(me, 1), :]
    return jnp.broadcast_to(row, (tokens, tokens)).T


def prepare(kv_refs, src_ref, lens_ref, pos_ref, kt_ref, va_ref, mask_ref, first, cached, tokens):
    width = cached + tokens
    own = own_columns(pos_ref, src_ref[0], tokens)
    slot = 0
    for ref in kv_refs:
        for part in range(ref.shape[0] // (2 * width)):
            base = part * 2 * width
            source = src_ref[first + slot]
            kt_ref[:, slot * width:(slot + 1) * width] = ref[base:base + width, :].T
            valid = lax.broadcasted_iota(jnp.int32, (cached, HD), 0) < lens_ref[source]
            stored = ref[base + width:base + width + cached, :]
            at = slot * width
            va_ref[at:at + cached, :HD] = jnp.where(valid, stored, jnp.zeros_like(stored))
            va_ref[at:at + cached, HD:] = jnp.where(valid, 1.0, 0.0).astype(jnp.bfloat16)
            va_ref[at + cached:at + width, :HD] = ref[base + width + cached:base + 2 * width, :]
            va_ref[at + cached:at + width, HD:] = jnp.ones((tokens, HD), jnp.bfloat16)
            seen = pos_ref[pl.ds(source, 1), :] <= own
            mask_ref[slot] = jnp.where(seen, 1.0, 0.0).astype(jnp.bfloat16)
            slot += 1
    return slot


def first_kernel(src_ref, lens_ref, q_ref, pos_ref, kv_ref, acc_ref, m_ref, kt_ref, va_ref, mask_ref, *, cached, tokens):
    @pl.when(pl.program_id(0) == 0)
    def _():
        prepare([kv_ref], src_ref, lens_ref, pos_ref, kt_ref, va_ref, mask_ref, 0, cached, tokens)

    scale = LOG2E * HD ** -0.5
    q = rows_of(q_ref)
    scores = jnp.dot(q, kt_ref[...], preferred_element_type=jnp.float32) * scale
    lane = lax.broadcasted_iota(jnp.int32, (1, cached), 1)
    bias = jnp.where(lane < lens_ref[src_ref[0]], 0.0, NEG)
    shown = jnp.concatenate([mask_ref[0].astype(jnp.float32)] * HG, 0) > 0.5
    scores = jnp.concatenate([scores[:, :cached] + bias, jnp.where(shown, scores[:, cached:], NEG)], 1)
    peak = jnp.max(scores, 1, keepdims=True)
    weights = jnp.exp2(scores - peak).astype(jnp.bfloat16)
    acc_ref[...] = jnp.dot(weights, va_ref[...], preferred_element_type=jnp.float32)
    for i in range(HG):
        m_ref[0, :, i:i + 1] = peak[i * tokens:(i + 1) * tokens, :]


def add_blocks(q_ref, m_ref, acc, kt_ref, va_ref, mask_ref, blocks, cached, tokens):
    width = cached + tokens
    scale = LOG2E * HD ** -0.5
    q = rows_of(q_ref)
    peak = jnp.concatenate([m_ref[0, :, i:i + 1] for i in range(HG)], 0)
    for b in range(blocks):
        at = b * width
        scores = jnp.dot(q, kt_ref[:, at:at + width], preferred_element_type=jnp.float32)
        weights = jnp.exp2(scores * scale - peak).astype(jnp.bfloat16)
        seen = jnp.concatenate([mask_ref[b]] * HG, 0)
        weights = jnp.concatenate([weights[:, :cached], weights[:, cached:] * seen], 1)
        acc = acc + jnp.dot(weights, va_ref[at:at + width, :], preferred_element_type=jnp.float32)
    return acc


def middle_kernel(src_ref, lens_ref, q_ref, pos_ref, m_ref, acc_in, *refs, first, count, cached, tokens):
    kv_refs, (acc_out, kt_ref, va_ref, mask_ref) = refs[:-4], refs[-4:]

    @pl.when(pl.program_id(0) == 0)
    def _():
        prepare(kv_refs, src_ref, lens_ref, pos_ref, kt_ref, va_ref, mask_ref, first, cached, tokens)

    acc_out[...] = add_blocks(q_ref, m_ref, acc_in[...], kt_ref, va_ref, mask_ref, count, cached, tokens)


def safe_rows(q_ref, acc_ref, peak_ref, everything, all_ref, sem, src_ref, lens_ref, pos_ref, cached, tokens):
    width = cached + tokens
    scale = LOG2E * HD ** -0.5
    slot = 0
    for ref in everything:
        for part in range(ref.shape[0] // (2 * width)):
            copy = pltpu.make_async_copy(ref.at[pl.ds(part * 2 * width, 2 * width)], all_ref.at[slot], sem)
            copy.start()
            copy.wait()
            slot += 1
    own = own_columns(pos_ref, src_ref[0], tokens)
    q = rows_of(q_ref)
    peak_ref[...] = jnp.full(peak_ref.shape, NEG, jnp.float32)
    acc_ref[...] = jnp.zeros(acc_ref.shape, jnp.float32)

    def step(b, carry):
        source = src_ref[b]
        scores = lax.dot_general(
            q, all_ref[b, :width, :], (((1,), (1,)), ((), ())), preferred_element_type=jnp.float32
        ) * scale
        lane = lax.broadcasted_iota(jnp.int32, (tokens, cached), 1)
        filled = jnp.where(lane < lens_ref[source], 1.0, 0.0)
        seen = jnp.where(pos_ref[pl.ds(source, 1), :] <= own, 1.0, 0.0)
        shown = jnp.concatenate([jnp.concatenate([filled, seen], 1)] * HG, 0) > 0.5
        scores = jnp.where(shown, scores, NEG)
        old = peak_ref[...]
        new = jnp.maximum(old, jnp.max(scores, 1, keepdims=True))
        weights = jnp.where(shown, jnp.exp2(scores - new[:, :1]), 0.0).astype(jnp.bfloat16)
        values = jnp.concatenate([all_ref[b, width:, :], jnp.ones((width, HD), jnp.bfloat16)], 1)
        factor = jnp.exp2(old - new)
        acc_ref[...] = acc_ref[...] * factor[:, :1] + jnp.dot(weights, values, preferred_element_type=jnp.float32)
        peak_ref[...] = new
        return carry

    lax.fori_loop(0, SIDE * SIDE, step, 0)


def last_kernel(src_ref, lens_ref, q_ref, pos_ref, m_ref, acc_in, *refs, first, count, parts, others, cached, tokens):
    kv_refs, others_refs = refs[:parts], refs[parts:parts + others]
    out_ref, kt_ref, va_ref, mask_ref, acc_ref, peak_ref, all_ref, sem = refs[parts + others:]

    @pl.when(pl.program_id(0) == 0)
    def _():
        prepare(kv_refs, src_ref, lens_ref, pos_ref, kt_ref, va_ref, mask_ref, first, cached, tokens)

    def finish(acc):
        result = (acc[:, :HD] / acc[:, HD:]).astype(jnp.bfloat16)
        for i in range(HG):
            out_ref[:, i * HD:(i + 1) * HD] = result[i * tokens:(i + 1) * tokens, :]

    acc = add_blocks(q_ref, m_ref, acc_in[...], kt_ref, va_ref, mask_ref, count, cached, tokens)
    finish(acc)
    bad = jnp.max(jnp.where(acc[:, HD:] < LIMIT, 0.0, 1.0)) > 0.5

    @pl.when(bad)
    def _():
        safe_rows(q_ref, acc_ref, peak_ref, others_refs, all_ref, sem, src_ref, lens_ref, pos_ref, cached, tokens)
        finish(acc_ref[...])


def shards(queries, new_keys, new_values, cache_keys, cache_values, cache_lens, new_pos):
    here = lax.axis_index("ctx")
    tokens, cached = new_keys.shape[0], cache_keys.shape[0]
    width = cached + tokens
    groups = queries.shape[1] // (HG * HD)
    rows = HG * tokens
    y, x = here // SIDE, here % SIDE
    offsets = jnp.array(ORDER, jnp.int32)
    sources = ((y + offsets[:, 0]) % SIDE) * SIDE + (x + offsets[:, 1]) % SIDE
    positions = new_pos.reshape(-1, tokens)

    smem = pl.BlockSpec(memory_space=pltpu.SMEM)
    whole = pl.BlockSpec(memory_space=pltpu.VMEM)
    head_block = pl.BlockSpec((tokens, HG * HD), lambda g: (0, g))
    acc_block = pl.BlockSpec((rows, 2 * HD), lambda g: (g, 0))
    peak_block = pl.BlockSpec((1, tokens, HD), lambda g: (g, 0, 0))
    acc_shape = jax.ShapeDtypeStruct((groups * rows, 2 * HD), jnp.float32)
    peak_shape = jax.ShapeDtypeStruct((groups, tokens, HD), jnp.float32)
    params = pltpu.CompilerParams(vmem_limit_bytes=VMEM)

    def scratch(blocks):
        return [
            pltpu.VMEM((HD, blocks * width), jnp.bfloat16),
            pltpu.VMEM((blocks * width, 2 * HD), jnp.bfloat16),
            pltpu.VMEM((blocks, tokens, tokens), jnp.bfloat16),
        ]

    def begin(own):
        return pl.pallas_call(
            functools.partial(first_kernel, cached=cached, tokens=tokens),
            grid=(groups,),
            in_specs=[smem, smem, head_block, whole, whole],
            out_specs=[acc_block, peak_block],
            out_shape=[acc_shape, peak_shape],
            scratch_shapes=scratch(1),
            compiler_params=params,
        )(sources, cache_lens, queries, positions, own)

    def add(acc, peak, parts, first, count):
        return pl.pallas_call(
            functools.partial(middle_kernel, first=first, count=count, cached=cached, tokens=tokens),
            grid=(groups,),
            in_specs=[smem, smem, head_block, whole, peak_block, acc_block] + [whole] * len(parts),
            out_specs=acc_block,
            out_shape=acc_shape,
            input_output_aliases={5: 0},
            scratch_shapes=scratch(count),
            compiler_params=params,
        )(sources, cache_lens, queries, positions, peak, acc, *parts)

    def end(acc, peak, parts, first, count, everything):
        return pl.pallas_call(
            functools.partial(last_kernel, first=first, count=count, parts=len(parts), others=len(everything),
                              cached=cached, tokens=tokens),
            grid=(groups,),
            in_specs=[smem, smem, head_block, whole, peak_block, acc_block] + [whole] * len(parts)
            + [whole] * len(everything),
            out_specs=head_block,
            out_shape=jax.ShapeDtypeStruct(queries.shape, jnp.bfloat16),
            scratch_shapes=scratch(count) + [
                pltpu.VMEM((rows, 2 * HD), jnp.float32),
                pltpu.VMEM((rows, HD), jnp.float32),
                pltpu.VMEM((SIDE * SIDE, 2 * width, HD), jnp.bfloat16),
                pltpu.SemaphoreType.DMA,
            ],
            compiler_params=params,
        )(sources, cache_lens, queries, positions, peak, acc, *parts, *everything)

    own = jnp.concatenate([cache_keys, new_keys, cache_values, new_values], 0)
    up, down = from_offset(own, -1, 0), from_offset(own, 1, 0)
    left, right = from_offset(own, 0, -1), from_offset(own, 0, 1)
    over_y, over_x = from_offset(own, 2, 0), from_offset(own, 0, 2)
    acc, peak = begin(own)

    acc, up, down, left, right = lax.optimization_barrier((acc, up, down, left, right))
    column = jnp.concatenate([up, down], 0)
    diag_left, diag_right = from_offset(column, 0, -1), from_offset(column, 0, 1)
    acc = add(acc, peak, [left, right, up, down], 1, 4)

    acc, over_y, over_x = lax.optimization_barrier((acc, over_y, over_x))
    far_left, far_right = from_offset(over_y, 0, -1), from_offset(over_y, 0, 1)
    far_up, far_down = from_offset(over_x, -1, 0), from_offset(over_x, 1, 0)
    opposite = from_offset(over_x, 2, 0)
    acc = add(acc, peak, [over_x, over_y], 5, 2)
    acc, diag_left, diag_right = lax.optimization_barrier((acc, diag_left, diag_right))
    acc = add(acc, peak, [diag_left, diag_right], 7, 4)
    last = [far_left, far_right, far_up, far_down, opposite]
    acc, *last = lax.optimization_barrier((acc, *last))
    everything = [own, left, right, up, down, over_x, over_y, diag_left, diag_right] + last
    return end(acc, peak, last, 11, 5, everything)


def solution(mesh):
    both = P(("batch", "ctx"), "head")
    placed = (both, both, both, both, both, P("batch"), P("batch"))
    return jax.shard_map(shards, mesh=mesh, in_specs=placed, out_specs=both, check_vma=False)
```

```python
import functools
import jax
import jax.numpy as jnp
from jax import lax
from jax.experimental import pallas as pl
from jax.experimental.pallas import tpu as pltpu
from jax.sharding import PartitionSpec as P

HD = 128
SIDE = 4
HG = 8
NEG = -1e30
LIMIT = 1e37
VMEM = 40 * 2**20
LOG2E = 1.4426950408889634

ORDER = (
    (0, 0),
    (-1, 0), (1, 0), (0, -1), (0, 1), (0, 2),
    (2, 0), (-1, -1), (1, -1), (-1, 1), (1, 1),
    (-1, 2), (1, 2), (2, 2), (2, -1), (2, 1),
)


def from_offset(block, dy, dx):
    route = []
    for y in range(SIDE):
        for x in range(SIDE):
            route.append((((y + dy) % SIDE) * SIDE + (x + dx) % SIDE, y * SIDE + x))
    return lax.ppermute(block, "ctx", route)


def rows_of(q_ref):
    return jnp.concatenate([q_ref[:, i * HD:(i + 1) * HD] for i in range(HG)], 0)


def source(slot):
    here = lax.axis_index("ctx")
    dy, dx = ORDER[slot]
    return ((here // SIDE + dy + SIDE) % SIDE) * SIDE + (here % SIDE + dx + SIDE) % SIDE


def pack_kernel(lens_ref, ck_ref, nk_ref, cv_ref, nv_ref, q_ref, pos_ref, out_ref, q_out, meta_ref,
                keys_ref, values_ref, posbuf_ref, lensbuf_ref, sems):
    cached, tokens = ck_ref.shape[0], nk_ref.shape[0]
    width = cached + tokens
    moves = [
        (ck_ref, keys_ref.at[pl.ds(0, cached)]),
        (nk_ref, keys_ref.at[pl.ds(cached, tokens)]),
        (cv_ref, values_ref),
        (nv_ref, out_ref.at[pl.ds(width + cached, tokens)]),
        (pos_ref, posbuf_ref),
        (q_ref, q_out),
        (lens_ref, lensbuf_ref),
    ]
    copies = [pltpu.make_async_copy(src, dst, sems.at[i]) for i, (src, dst) in enumerate(moves)]
    for copy in copies:
        copy.start()
    copies[6].wait()
    for slot in range(len(ORDER)):
        meta_ref[len(ORDER) + slot:len(ORDER) + slot + 1, :] = jnp.full((1, HD), lensbuf_ref[source(slot)], jnp.int32)
    copies[0].wait()
    copies[1].wait()
    for t in range(width // HD):
        out_ref[t * HD:(t + 1) * HD, :] = keys_ref[t * HD:(t + 1) * HD, :].T
    copies[2].wait()
    valid = lax.broadcasted_iota(jnp.int32, (cached, HD), 0) < meta_ref[len(ORDER):len(ORDER) + 1, :]
    stored = values_ref[...]
    out_ref[width:width + cached, :] = jnp.where(valid, stored, jnp.zeros_like(stored))
    copies[4].wait()
    for slot in range(len(ORDER)):
        meta_ref[slot:slot + 1, :] = posbuf_ref[pl.ds(source(slot), 1), :]
    copies[3].wait()
    copies[5].wait()


def blocks_of(refs, width):
    return [(ref, part * 2 * width) for ref in refs for part in range(ref.shape[0] // (2 * width))]


def keys_at(tiles):
    return jnp.concatenate([ref[base + t * HD:base + (t + 1) * HD, :] for ref, base, _, t in tiles], 1)


def values_at(tiles, ones_ref, cached, tokens):
    values, ones = [], []
    for ref, base, b, t in tiles:
        at = base + cached + tokens + t * HD
        values.append(ref[at:at + HD, :])
        ones.append(ones_ref[b, t * HD:(t + 1) * HD, :] if t < cached // HD else jnp.ones((HD, HD), jnp.bfloat16))
    return jnp.concatenate([jnp.concatenate(values, 0), jnp.concatenate(ones, 0)], 1)


def fill_ones(meta_ref, ones_ref, first, count, cached):
    for b in range(count):
        row = len(ORDER) + first + b
        valid = lax.broadcasted_iota(jnp.int32, (cached, HD), 0) < meta_ref[row:row + 1, :]
        ones_ref[b] = jnp.where(valid, 1.0, 0.0).astype(jnp.bfloat16)


def first_kernel(q_ref, meta_ref, kv_ref, acc_ref, m_ref, mask_ref, ones_ref, *, cached, tokens):
    width = cached + tokens

    @pl.when(pl.program_id(0) == 0)
    def _():
        fill_ones(meta_ref, ones_ref, 0, 1, cached)
        own = jnp.broadcast_to(meta_ref[0:1, :], (tokens, tokens)).T
        for slot in range(len(ORDER)):
            seen = meta_ref[slot:slot + 1, :] <= own
            mask_ref[slot] = jnp.where(seen, 1.0, 0.0).astype(jnp.bfloat16)

    scale = LOG2E * HD ** -0.5
    q = rows_of(q_ref)
    tiles = [(kv_ref, 0, 0, t) for t in range(width // HD)]
    scores = jnp.dot(q, keys_at(tiles), preferred_element_type=jnp.float32) * scale
    lane = lax.broadcasted_iota(jnp.int32, (1, cached), 1)
    length = jnp.concatenate([meta_ref[len(ORDER):len(ORDER) + 1, :]] * (cached // HD), 1)
    bias = jnp.where(lane < length, 0.0, NEG)
    shown = jnp.concatenate([mask_ref[0].astype(jnp.float32)] * HG, 0) > 0.5
    scores = jnp.concatenate([scores[:, :cached] + bias, jnp.where(shown, scores[:, cached:], NEG)], 1)
    peak = jnp.max(scores, 1, keepdims=True)
    weights = jnp.exp2(scores - peak).astype(jnp.bfloat16)
    values = values_at(tiles, ones_ref, cached, tokens)
    acc_ref[...] = jnp.dot(weights, values, preferred_element_type=jnp.float32)
    for i in range(HG):
        m_ref[0, :, i:i + 1] = peak[i * tokens:(i + 1) * tokens, :]


def add_blocks(q_ref, m_ref, mask_ref, acc, kv_refs, ones_ref, first, cached, tokens):
    width = cached + tokens
    scale = LOG2E * HD ** -0.5
    full = cached // HD
    q = rows_of(q_ref)
    peak = jnp.concatenate([m_ref[0, :, i:i + 1] for i in range(HG)], 0)
    blocks = [(ref, base, b) for b, (ref, base) in enumerate(blocks_of(kv_refs, width))]
    for p in range(0, len(blocks), 2):
        pair = blocks[p:p + 2]
        tiles = [block + (t,) for block in pair for t in range(full)]
        tiles += [block + (t,) for block in pair for t in range(full, width // HD)]
        scores = jnp.dot(q, keys_at(tiles), preferred_element_type=jnp.float32)
        weights = jnp.exp2(scores * scale - peak).astype(jnp.bfloat16)
        at = len(pair) * cached
        parts = [weights[:, :at]]
        for i, (_, _, b) in enumerate(pair):
            seen = jnp.concatenate([mask_ref[first + b]] * HG, 0)
            parts.append(weights[:, at + i * tokens:at + (i + 1) * tokens] * seen)
        values = values_at(tiles, ones_ref, cached, tokens)
        acc = acc + jnp.dot(jnp.concatenate(parts, 1), values, preferred_element_type=jnp.float32)
    return acc


def middle_kernel(meta_ref, q_ref, m_ref, mask_ref, acc_in, *refs, first, count, cached, tokens):
    kv_refs, (acc_out, ones_ref) = refs[:-2], refs[-2:]

    @pl.when(pl.program_id(0) == 0)
    def _():
        fill_ones(meta_ref, ones_ref, first, count, cached)

    acc_out[...] = add_blocks(q_ref, m_ref, mask_ref, acc_in[...], kv_refs, ones_ref, first, cached, tokens)


def safe_rows(q_ref, mask_ref, acc_ref, peak_ref, everything, all_ref, sem, meta_ref, cached, tokens):
    width = cached + tokens
    scale = LOG2E * HD ** -0.5
    for slot, (ref, base) in enumerate(blocks_of(everything, width)):
        copy = pltpu.make_async_copy(ref.at[pl.ds(base, 2 * width)], all_ref.at[slot], sem)
        copy.start()
        copy.wait()
    q = rows_of(q_ref)
    peak_ref[...] = jnp.full(peak_ref.shape, NEG, jnp.float32)
    acc_ref[...] = jnp.zeros(acc_ref.shape, jnp.float32)

    def step(b, carry):
        keys = jnp.concatenate([all_ref[b, t * HD:(t + 1) * HD, :] for t in range(width // HD)], 1)
        scores = jnp.dot(q, keys, preferred_element_type=jnp.float32) * scale
        lane = lax.broadcasted_iota(jnp.int32, (tokens, cached), 1)
        length = jnp.concatenate([meta_ref[pl.ds(len(ORDER) + b, 1), :]] * (cached // HD), 1)
        filled = jnp.where(lane < length, 1.0, 0.0)
        seen = mask_ref[b].astype(jnp.float32)
        shown = jnp.concatenate([jnp.concatenate([filled, seen], 1)] * HG, 0) > 0.5
        scores = jnp.where(shown, scores, NEG)
        old = peak_ref[...]
        new = jnp.maximum(old, jnp.max(scores, 1, keepdims=True))
        weights = jnp.where(shown, jnp.exp2(scores - new[:, :1]), 0.0).astype(jnp.bfloat16)
        values = jnp.concatenate([all_ref[b, width:, :], jnp.ones((width, HD), jnp.bfloat16)], 1)
        factor = jnp.exp2(old - new)
        acc_ref[...] = acc_ref[...] * factor[:, :1] + jnp.dot(weights, values, preferred_element_type=jnp.float32)
        peak_ref[...] = new
        return carry

    lax.fori_loop(0, len(ORDER), step, 0)


def last_kernel(meta_ref, q_ref, m_ref, mask_ref, acc_in, *refs, first, count, parts, others, cached, tokens):
    kv_refs, others_refs = refs[:parts], refs[parts:parts + others]
    out_ref, ones_ref, acc_ref, peak_ref, all_ref, sem = refs[parts + others:]

    @pl.when(pl.program_id(0) == 0)
    def _():
        fill_ones(meta_ref, ones_ref, first, count, cached)

    def finish(acc):
        result = (acc[:, :HD] / acc[:, HD:]).astype(jnp.bfloat16)
        for i in range(HG):
            out_ref[:, i * HD:(i + 1) * HD] = result[i * tokens:(i + 1) * tokens, :]

    acc = add_blocks(q_ref, m_ref, mask_ref, acc_in[...], kv_refs, ones_ref, first, cached, tokens)
    finish(acc)
    bad = jnp.max(jnp.where(acc[:, HD:] < LIMIT, 0.0, 1.0)) > 0.5

    @pl.when(bad)
    def _():
        safe_rows(q_ref, mask_ref, acc_ref, peak_ref, others_refs, all_ref, sem, meta_ref, cached, tokens)
        finish(acc_ref[...])


def shards(queries, new_keys, new_values, cache_keys, cache_values, cache_lens, new_pos):
    tokens, cached = new_keys.shape[0], cache_keys.shape[0]
    width = cached + tokens
    groups = queries.shape[1] // (HG * HD)
    rows = HG * tokens
    positions = new_pos.reshape(-1, tokens)

    whole = pl.BlockSpec(memory_space=pltpu.VMEM)
    head_block = pl.BlockSpec((tokens, HG * HD), lambda g: (0, g))
    acc_block = pl.BlockSpec((rows, 2 * HD), lambda g: (g, 0))
    peak_block = pl.BlockSpec((1, tokens, HD), lambda g: (g, 0, 0))
    acc_shape = jax.ShapeDtypeStruct((groups * rows, 2 * HD), jnp.float32)
    peak_shape = jax.ShapeDtypeStruct((groups, tokens, HD), jnp.float32)
    mask_shape = jax.ShapeDtypeStruct((len(ORDER), tokens, tokens), jnp.bfloat16)
    params = pltpu.CompilerParams(vmem_limit_bytes=VMEM)
    cost = pl.CostEstimate(flops=1, bytes_accessed=1, transcendentals=0)

    def ones(blocks):
        return pltpu.VMEM((blocks, cached, HD), jnp.bfloat16)

    def pack():
        return pl.pallas_call(
            pack_kernel,
            in_specs=[pl.BlockSpec(memory_space=pltpu.HBM)] * 7,
            out_specs=[whole] * 3,
            out_shape=[
                pltpu.VMEM((2 * width, HD), jnp.bfloat16),
                pltpu.VMEM(queries.shape, jnp.bfloat16),
                pltpu.VMEM((2 * len(ORDER), tokens), jnp.int32),
            ],
            scratch_shapes=[
                pltpu.VMEM((width, HD), jnp.bfloat16),
                pltpu.VMEM((cached, HD), jnp.bfloat16),
                pltpu.VMEM(positions.shape, jnp.int32),
                pltpu.SMEM(cache_lens.shape, jnp.int32),
                pltpu.SemaphoreType.DMA((7,)),
            ],
            compiler_params=params,
            cost_estimate=cost,
        )(*[
            pltpu.with_memory_space_constraint(part, pltpu.HBM)
            for part in (cache_lens, cache_keys, new_keys, cache_values, new_values, queries, positions)
        ])

    def begin(own):
        return pl.pallas_call(
            functools.partial(first_kernel, cached=cached, tokens=tokens),
            grid=(groups,),
            in_specs=[head_block, whole, whole],
            out_specs=[acc_block, peak_block, whole],
            out_shape=[acc_shape, peak_shape, mask_shape],
            scratch_shapes=[ones(1)],
            compiler_params=params,
            cost_estimate=cost,
        )(query, meta, own)

    def add(acc, peak, mask, parts, first, count):
        return pl.pallas_call(
            functools.partial(middle_kernel, first=first, count=count, cached=cached, tokens=tokens),
            grid=(groups,),
            in_specs=[whole, head_block, peak_block, whole, acc_block] + [whole] * len(parts),
            out_specs=acc_block,
            out_shape=acc_shape,
            input_output_aliases={4: 0},
            scratch_shapes=[ones(count)],
            compiler_params=params,
            cost_estimate=cost,
        )(meta, query, peak, mask, acc, *parts)

    def end(acc, peak, mask, parts, first, count, everything):
        return pl.pallas_call(
            functools.partial(last_kernel, first=first, count=count, parts=len(parts), others=len(everything),
                              cached=cached, tokens=tokens),
            grid=(groups,),
            in_specs=[whole, head_block, peak_block, whole, acc_block] + [whole] * (len(parts) + len(everything)),
            out_specs=head_block,
            out_shape=jax.ShapeDtypeStruct(queries.shape, jnp.bfloat16),
            scratch_shapes=[
                ones(count),
                pltpu.VMEM((rows, 2 * HD), jnp.float32),
                pltpu.VMEM((rows, HD), jnp.float32),
                pltpu.VMEM((len(ORDER), 2 * width, HD), jnp.bfloat16),
                pltpu.SemaphoreType.DMA,
            ],
            compiler_params=params,
            cost_estimate=cost,
        )(meta, query, peak, mask, acc, *parts, *everything)

    tie = lax.optimization_barrier
    own, query, meta = pack()
    up, down = from_offset(own, -1, 0), from_offset(own, 1, 0)
    left, right = from_offset(own, 0, -1), from_offset(own, 0, 1)
    over_x = from_offset(own, 0, 2)
    acc, peak, mask = begin(own)

    acc, up, down = tie((acc, up, down))
    acc = add(acc, peak, mask, [up, down], 1, 2)

    acc, own_later, up, down, left, right, over_x = tie((acc, own, up, down, left, right, over_x))
    column = jnp.concatenate([up, down], 0)
    diag_left, diag_right = from_offset(column, 0, -1), from_offset(column, 0, 1)
    over_y = from_offset(own_later, 2, 0)
    far_up, far_down = from_offset(over_x, -1, 0), from_offset(over_x, 1, 0)
    acc = add(acc, peak, mask, [left, right, over_x], 3, 3)

    acc, over_y, over_x_later = tie((acc, over_y, over_x))
    far_left, far_right = from_offset(over_y, 0, -1), from_offset(over_y, 0, 1)
    opposite = from_offset(over_x_later, 2, 0)
    acc, diag_left, diag_right, over_y_later = tie((acc, diag_left, diag_right, over_y))
    acc = add(acc, peak, mask, [over_y_later, diag_left, diag_right], 6, 5)

    last = [far_up, far_down, opposite, far_left, far_right]
    acc, *last = tie((acc, *last))
    everything = [own, up, down, left, right, over_x, over_y, diag_left, diag_right]
    return end(acc, peak, mask, last, 11, 5, everything + last)


def solution(mesh):
    both = P(("batch", "ctx"), "head")
    placed = (both, both, both, both, both, P("batch"), P("batch"))
    return jax.shard_map(shards, mesh=mesh, in_specs=placed, out_specs=both, check_vma=False)
```

```python
import functools
import jax
import jax.numpy as jnp
from jax import lax
from jax.experimental import pallas as pl
from jax.experimental.pallas import tpu as pltpu
from jax.sharding import PartitionSpec as P

HD = 128
SIDE = 4
HG = 8
NEG = -1e30
LIMIT = 1e37
VMEM = 40 * 2**20
LOG2E = 1.4426950408889634

ORDER = (
    (0, 0),
    (-1, 0), (1, 0), (0, -1), (0, 1), (0, 2),
    (2, 0), (-1, 2), (1, 2), (-1, -1), (1, -1), (-1, 1), (1, 1),
    (2, 2), (2, -1), (2, 1),
)


def from_offset(block, dy, dx):
    route = []
    for y in range(SIDE):
        for x in range(SIDE):
            route.append((((y + dy) % SIDE) * SIDE + (x + dx) % SIDE, y * SIDE + x))
    return lax.ppermute(block, "ctx", route)


def rows_of(q_ref):
    return jnp.concatenate([q_ref[:, i * HD:(i + 1) * HD] for i in range(HG)], 0)


def source(slot):
    here = lax.axis_index("ctx")
    dy, dx = ORDER[slot]
    return ((here // SIDE + dy + SIDE) % SIDE) * SIDE + (here % SIDE + dx + SIDE) % SIDE


def pack_kernel(lens_ref, ck_ref, nk_ref, cv_ref, nv_ref, q_ref, pos_ref, out_ref, q_out, meta_ref,
                keys_ref, values_ref, posbuf_ref, lensbuf_ref, sems):
    cached, tokens = ck_ref.shape[0], nk_ref.shape[0]
    width = cached + tokens
    moves = [
        (ck_ref, keys_ref.at[pl.ds(0, cached)]),
        (nk_ref, keys_ref.at[pl.ds(cached, tokens)]),
        (cv_ref, values_ref),
        (nv_ref, out_ref.at[pl.ds(width + cached, tokens)]),
        (pos_ref, posbuf_ref),
        (q_ref, q_out),
        (lens_ref, lensbuf_ref),
    ]
    copies = [pltpu.make_async_copy(src, dst, sems.at[i]) for i, (src, dst) in enumerate(moves)]
    for copy in copies:
        copy.start()
    copies[6].wait()
    for slot in range(len(ORDER)):
        meta_ref[len(ORDER) + slot:len(ORDER) + slot + 1, :] = jnp.full((1, HD), lensbuf_ref[source(slot)], jnp.int32)
    copies[0].wait()
    copies[1].wait()
    for t in range(width // HD):
        out_ref[t * HD:(t + 1) * HD, :] = keys_ref[t * HD:(t + 1) * HD, :].T
    copies[2].wait()
    valid = lax.broadcasted_iota(jnp.int32, (cached, HD), 0) < meta_ref[len(ORDER):len(ORDER) + 1, :]
    stored = values_ref[...]
    out_ref[width:width + cached, :] = jnp.where(valid, stored, jnp.zeros_like(stored))
    copies[4].wait()
    for slot in range(len(ORDER)):
        meta_ref[slot:slot + 1, :] = posbuf_ref[pl.ds(source(slot), 1), :]
    copies[3].wait()
    copies[5].wait()


def blocks_of(refs, width):
    return [(ref, part * 2 * width) for ref in refs for part in range(ref.shape[0] // (2 * width))]


def keys_at(tiles):
    return jnp.concatenate([ref[base + t * HD:base + (t + 1) * HD, :] for ref, base, _, t in tiles], 1)


def values_at(tiles, ones_ref, cached, tokens):
    values, ones = [], []
    for ref, base, b, t in tiles:
        at = base + cached + tokens + t * HD
        values.append(ref[at:at + HD, :])
        ones.append(ones_ref[b, t * HD:(t + 1) * HD, :] if t < cached // HD else jnp.ones((HD, HD), jnp.bfloat16))
    return jnp.concatenate([jnp.concatenate(values, 0), jnp.concatenate(ones, 0)], 1)


def fill_ones(meta_ref, ones_ref, first, count, cached):
    for b in range(count):
        row = len(ORDER) + first + b
        valid = lax.broadcasted_iota(jnp.int32, (cached, HD), 0) < meta_ref[row:row + 1, :]
        ones_ref[b] = jnp.where(valid, 1.0, 0.0).astype(jnp.bfloat16)


def first_kernel(q_ref, meta_ref, kv_ref, acc_ref, m_ref, mask_ref, ones_ref, *, cached, tokens):
    width = cached + tokens

    @pl.when(pl.program_id(0) == 0)
    def _():
        fill_ones(meta_ref, ones_ref, 0, 1, cached)
        own = jnp.broadcast_to(meta_ref[0:1, :], (tokens, tokens)).T
        for slot in range(len(ORDER)):
            seen = meta_ref[slot:slot + 1, :] <= own
            mask_ref[slot] = jnp.where(seen, 1.0, 0.0).astype(jnp.bfloat16)

    scale = LOG2E * HD ** -0.5
    q = rows_of(q_ref)
    tiles = [(kv_ref, 0, 0, t) for t in range(width // HD)]
    scores = jnp.dot(q, keys_at(tiles), preferred_element_type=jnp.float32) * scale
    lane = lax.broadcasted_iota(jnp.int32, (1, cached), 1)
    length = jnp.concatenate([meta_ref[len(ORDER):len(ORDER) + 1, :]] * (cached // HD), 1)
    bias = jnp.where(lane < length, 0.0, NEG)
    shown = jnp.concatenate([mask_ref[0].astype(jnp.float32)] * HG, 0) > 0.5
    scores = jnp.concatenate([scores[:, :cached] + bias, jnp.where(shown, scores[:, cached:], NEG)], 1)
    peak = jnp.max(scores, 1, keepdims=True)
    weights = jnp.exp2(scores - peak).astype(jnp.bfloat16)
    values = values_at(tiles, ones_ref, cached, tokens)
    acc_ref[...] = jnp.dot(weights, values, preferred_element_type=jnp.float32)
    for i in range(HG):
        m_ref[0, :, i:i + 1] = peak[i * tokens:(i + 1) * tokens, :]


def add_blocks(q_ref, m_ref, mask_ref, acc, kv_refs, ones_ref, first, cached, tokens):
    width = cached + tokens
    scale = LOG2E * HD ** -0.5
    full = cached // HD
    q = rows_of(q_ref)
    peak = jnp.concatenate([m_ref[0, :, i:i + 1] for i in range(HG)], 0)
    blocks = [(ref, base, b) for b, (ref, base) in enumerate(blocks_of(kv_refs, width))]
    for p in range(0, len(blocks), 2):
        pair = blocks[p:p + 2]
        tiles = [block + (t,) for block in pair for t in range(full)]
        tiles += [block + (t,) for block in pair for t in range(full, width // HD)]
        scores = jnp.dot(q, keys_at(tiles), preferred_element_type=jnp.float32)
        weights = jnp.exp2(scores * scale - peak).astype(jnp.bfloat16)
        at = len(pair) * cached
        parts = [weights[:, :at]]
        for i, (_, _, b) in enumerate(pair):
            seen = jnp.concatenate([mask_ref[first + b]] * HG, 0)
            parts.append(weights[:, at + i * tokens:at + (i + 1) * tokens] * seen)
        values = values_at(tiles, ones_ref, cached, tokens)
        acc = acc + jnp.dot(jnp.concatenate(parts, 1), values, preferred_element_type=jnp.float32)
    return acc


def middle_kernel(meta_ref, q_ref, m_ref, mask_ref, acc_in, *refs, first, count, cached, tokens):
    kv_refs, (acc_out, ones_ref) = refs[:-2], refs[-2:]

    @pl.when(pl.program_id(0) == 0)
    def _():
        fill_ones(meta_ref, ones_ref, first, count, cached)

    acc_out[...] = add_blocks(q_ref, m_ref, mask_ref, acc_in[...], kv_refs, ones_ref, first, cached, tokens)


def safe_rows(q_ref, mask_ref, acc_ref, peak_ref, everything, all_ref, sem, meta_ref, cached, tokens):
    width = cached + tokens
    scale = LOG2E * HD ** -0.5
    for slot, (ref, base) in enumerate(blocks_of(everything, width)):
        copy = pltpu.make_async_copy(ref.at[pl.ds(base, 2 * width)], all_ref.at[slot], sem)
        copy.start()
        copy.wait()
    q = rows_of(q_ref)
    peak_ref[...] = jnp.full(peak_ref.shape, NEG, jnp.float32)
    acc_ref[...] = jnp.zeros(acc_ref.shape, jnp.float32)

    def step(b, carry):
        keys = jnp.concatenate([all_ref[b, t * HD:(t + 1) * HD, :] for t in range(width // HD)], 1)
        scores = jnp.dot(q, keys, preferred_element_type=jnp.float32) * scale
        lane = lax.broadcasted_iota(jnp.int32, (tokens, cached), 1)
        length = jnp.concatenate([meta_ref[pl.ds(len(ORDER) + b, 1), :]] * (cached // HD), 1)
        filled = jnp.where(lane < length, 1.0, 0.0)
        seen = mask_ref[b].astype(jnp.float32)
        shown = jnp.concatenate([jnp.concatenate([filled, seen], 1)] * HG, 0) > 0.5
        scores = jnp.where(shown, scores, NEG)
        old = peak_ref[...]
        new = jnp.maximum(old, jnp.max(scores, 1, keepdims=True))
        weights = jnp.where(shown, jnp.exp2(scores - new[:, :1]), 0.0).astype(jnp.bfloat16)
        values = jnp.concatenate([all_ref[b, width:, :], jnp.ones((width, HD), jnp.bfloat16)], 1)
        factor = jnp.exp2(old - new)
        acc_ref[...] = acc_ref[...] * factor[:, :1] + jnp.dot(weights, values, preferred_element_type=jnp.float32)
        peak_ref[...] = new
        return carry

    lax.fori_loop(0, len(ORDER), step, 0)


def last_kernel(meta_ref, q_ref, m_ref, mask_ref, acc_in, *refs, first, count, parts, others, cached, tokens):
    kv_refs, others_refs = refs[:parts], refs[parts:parts + others]
    out_ref, ones_ref, acc_ref, peak_ref, all_ref, sem = refs[parts + others:]

    @pl.when(pl.program_id(0) == 0)
    def _():
        fill_ones(meta_ref, ones_ref, first, count, cached)

    def finish(acc):
        result = (acc[:, :HD] / acc[:, HD:]).astype(jnp.bfloat16)
        for i in range(HG):
            out_ref[:, i * HD:(i + 1) * HD] = result[i * tokens:(i + 1) * tokens, :]

    acc = add_blocks(q_ref, m_ref, mask_ref, acc_in[...], kv_refs, ones_ref, first, cached, tokens)
    finish(acc)
    bad = jnp.max(jnp.where(acc[:, HD:] < LIMIT, 0.0, 1.0)) > 0.5

    @pl.when(bad)
    def _():
        safe_rows(q_ref, mask_ref, acc_ref, peak_ref, others_refs, all_ref, sem, meta_ref, cached, tokens)
        finish(acc_ref[...])


def shards(queries, new_keys, new_values, cache_keys, cache_values, cache_lens, new_pos):
    tokens, cached = new_keys.shape[0], cache_keys.shape[0]
    width = cached + tokens
    groups = queries.shape[1] // (HG * HD)
    rows = HG * tokens
    positions = new_pos.reshape(-1, tokens)

    whole = pl.BlockSpec(memory_space=pltpu.VMEM)
    head_block = pl.BlockSpec((tokens, HG * HD), lambda g: (0, g))
    acc_block = pl.BlockSpec((rows, 2 * HD), lambda g: (g, 0))
    peak_block = pl.BlockSpec((1, tokens, HD), lambda g: (g, 0, 0))
    acc_shape = jax.ShapeDtypeStruct((groups * rows, 2 * HD), jnp.float32)
    peak_shape = jax.ShapeDtypeStruct((groups, tokens, HD), jnp.float32)
    mask_shape = jax.ShapeDtypeStruct((len(ORDER), tokens, tokens), jnp.bfloat16)
    params = pltpu.CompilerParams(vmem_limit_bytes=VMEM)
    cost = pl.CostEstimate(flops=1, bytes_accessed=1, transcendentals=0)

    def ones(blocks):
        return pltpu.VMEM((blocks, cached, HD), jnp.bfloat16)

    def pack():
        return pl.pallas_call(
            pack_kernel,
            in_specs=[pl.BlockSpec(memory_space=pltpu.HBM)] * 7,
            out_specs=[whole] * 3,
            out_shape=[
                pltpu.VMEM((2 * width, HD), jnp.bfloat16),
                pltpu.VMEM(queries.shape, jnp.bfloat16),
                pltpu.VMEM((2 * len(ORDER), tokens), jnp.int32),
            ],
            scratch_shapes=[
                pltpu.VMEM((width, HD), jnp.bfloat16),
                pltpu.VMEM((cached, HD), jnp.bfloat16),
                pltpu.VMEM(positions.shape, jnp.int32),
                pltpu.SMEM(cache_lens.shape, jnp.int32),
                pltpu.SemaphoreType.DMA((7,)),
            ],
            compiler_params=params,
            cost_estimate=cost,
        )(*[
            pltpu.with_memory_space_constraint(part, pltpu.HBM)
            for part in (cache_lens, cache_keys, new_keys, cache_values, new_values, queries, positions)
        ])

    def begin(own):
        return pl.pallas_call(
            functools.partial(first_kernel, cached=cached, tokens=tokens),
            grid=(groups,),
            in_specs=[head_block, whole, whole],
            out_specs=[acc_block, peak_block, whole],
            out_shape=[acc_shape, peak_shape, mask_shape],
            scratch_shapes=[ones(1)],
            compiler_params=params,
            cost_estimate=cost,
        )(query, meta, own)

    def add(acc, peak, mask, parts, first, count):
        return pl.pallas_call(
            functools.partial(middle_kernel, first=first, count=count, cached=cached, tokens=tokens),
            grid=(groups,),
            in_specs=[whole, head_block, peak_block, whole, acc_block] + [whole] * len(parts),
            out_specs=acc_block,
            out_shape=acc_shape,
            input_output_aliases={4: 0},
            scratch_shapes=[ones(count)],
            compiler_params=params,
            cost_estimate=cost,
        )(meta, query, peak, mask, acc, *parts)

    def end(acc, peak, mask, parts, first, count, everything):
        return pl.pallas_call(
            functools.partial(last_kernel, first=first, count=count, parts=len(parts), others=len(everything),
                              cached=cached, tokens=tokens),
            grid=(groups,),
            in_specs=[whole, head_block, peak_block, whole, acc_block] + [whole] * (len(parts) + len(everything)),
            out_specs=head_block,
            out_shape=jax.ShapeDtypeStruct(queries.shape, jnp.bfloat16),
            scratch_shapes=[
                ones(count),
                pltpu.VMEM((rows, 2 * HD), jnp.float32),
                pltpu.VMEM((rows, HD), jnp.float32),
                pltpu.VMEM((len(ORDER), 2 * width, HD), jnp.bfloat16),
                pltpu.SemaphoreType.DMA,
            ],
            compiler_params=params,
            cost_estimate=cost,
        )(meta, query, peak, mask, acc, *parts, *everything)

    tie = lax.optimization_barrier
    own, query, meta = pack()
    up, down = from_offset(own, -1, 0), from_offset(own, 1, 0)
    left, right = from_offset(own, 0, -1), from_offset(own, 0, 1)
    over_x = from_offset(own, 0, 2)
    acc, peak, mask = begin(own)

    acc, up, down, own_later = tie((acc, up, down, own))
    over_y = from_offset(own_later, 2, 0)
    acc = add(acc, peak, mask, [up, down], 1, 2)

    acc, up, down, left, right, over_x, over_y = tie((acc, up, down, left, right, over_x, over_y))
    column = jnp.concatenate([up, down], 0)
    diag_left, diag_right = from_offset(column, 0, -1), from_offset(column, 0, 1)
    far_up, far_down = from_offset(over_x, -1, 0), from_offset(over_x, 1, 0)
    acc = add(acc, peak, mask, [left, right, over_x, over_y], 3, 4)

    acc, far_up, far_down, over_x_later = tie((acc, far_up, far_down, over_x))
    opposite = from_offset(over_x_later, 2, 0)
    acc = add(acc, peak, mask, [far_up, far_down], 7, 2)

    acc, diag_left, diag_right, over_y_later = tie((acc, diag_left, diag_right, over_y))
    far_left, far_right = from_offset(over_y_later, 0, -1), from_offset(over_y_later, 0, 1)
    acc = add(acc, peak, mask, [diag_left, diag_right], 9, 4)

    last = [opposite, far_left, far_right]
    acc, *last = tie((acc, *last))
    everything = [own, up, down, left, right, over_x, over_y, far_up, far_down, diag_left, diag_right]
    return end(acc, peak, mask, last, 13, 3, everything + last)


def solution(mesh):
    both = P(("batch", "ctx"), "head")
    placed = (both, both, both, both, both, P("batch"), P("batch"))
    return jax.shard_map(shards, mesh=mesh, in_specs=placed, out_specs=both, check_vma=False)
```

```python
import functools
import jax
import jax.numpy as jnp
from jax import lax
from jax.experimental import pallas as pl
from jax.experimental.pallas import tpu as pltpu
from jax.sharding import PartitionSpec as P

HD = 128
SIDE = 4
HG = 16
NEG = -1e30
LIMIT = 1e37
VMEM = 40 * 2**20
LOG2E = 1.4426950408889634

ORDER = (
    (0, 0),
    (-1, 0), (1, 0), (0, -1), (0, 1), (0, 2),
    (2, 0), (-1, 2), (1, 2), (-1, -1), (1, -1), (-1, 1), (1, 1),
    (2, 2), (2, -1), (2, 1),
)


def from_offset(block, dy, dx):
    route = []
    for y in range(SIDE):
        for x in range(SIDE):
            route.append((((y + dy) % SIDE) * SIDE + (x + dx) % SIDE, y * SIDE + x))
    return lax.ppermute(block, "ctx", route)


def rows_of(q_ref):
    return jnp.concatenate([q_ref[:, i * HD:(i + 1) * HD] for i in range(HG)], 0)


def source(slot):
    here = lax.axis_index("ctx")
    dy, dx = ORDER[slot]
    return ((here // SIDE + dy + SIDE) % SIDE) * SIDE + (here % SIDE + dx + SIDE) % SIDE


def pack_kernel(lens_ref, ck_ref, nk_ref, cv_ref, nv_ref, q_ref, pos_ref, out_ref, q_out, meta_ref,
                keys_ref, values_ref, posbuf_ref, lensbuf_ref, sems):
    cached, tokens = ck_ref.shape[0], nk_ref.shape[0]
    width = cached + tokens
    moves = [
        (ck_ref, keys_ref.at[pl.ds(0, cached)]),
        (nk_ref, keys_ref.at[pl.ds(cached, tokens)]),
        (cv_ref, values_ref),
        (nv_ref, out_ref.at[pl.ds(width + cached, tokens)]),
        (pos_ref, posbuf_ref),
        (q_ref, q_out),
        (lens_ref, lensbuf_ref),
    ]
    copies = [pltpu.make_async_copy(src, dst, sems.at[i]) for i, (src, dst) in enumerate(moves)]
    for copy in copies:
        copy.start()
    copies[6].wait()
    for slot in range(len(ORDER)):
        meta_ref[len(ORDER) + slot:len(ORDER) + slot + 1, :] = jnp.full((1, HD), lensbuf_ref[source(slot)], jnp.int32)
    copies[0].wait()
    copies[1].wait()
    for t in range(width // HD):
        out_ref[t * HD:(t + 1) * HD, :] = keys_ref[t * HD:(t + 1) * HD, :].T
    copies[2].wait()
    valid = lax.broadcasted_iota(jnp.int32, (cached, HD), 0) < meta_ref[len(ORDER):len(ORDER) + 1, :]
    stored = values_ref[...]
    out_ref[width:width + cached, :] = jnp.where(valid, stored, jnp.zeros_like(stored))
    copies[4].wait()
    for slot in range(len(ORDER)):
        meta_ref[slot:slot + 1, :] = posbuf_ref[pl.ds(source(slot), 1), :]
    copies[3].wait()
    copies[5].wait()


def blocks_of(refs, width):
    return [(ref, part * 2 * width) for ref in refs for part in range(ref.shape[0] // (2 * width))]


def keys_at(tiles):
    return jnp.concatenate([ref[base + t * HD:base + (t + 1) * HD, :] for ref, base, _, t in tiles], 1)


def values_at(tiles, ones_ref, cached, tokens):
    values, ones = [], []
    for ref, base, b, t in tiles:
        at = base + cached + tokens + t * HD
        values.append(ref[at:at + HD, :])
        ones.append(ones_ref[b, t * HD:(t + 1) * HD, :] if t < cached // HD else jnp.ones((HD, HD), jnp.bfloat16))
    return jnp.concatenate([jnp.concatenate(values, 0), jnp.concatenate(ones, 0)], 1)


def fill_ones(meta_ref, ones_ref, first, count, cached):
    for b in range(count):
        row = len(ORDER) + first + b
        valid = lax.broadcasted_iota(jnp.int32, (cached, HD), 0) < meta_ref[row:row + 1, :]
        ones_ref[b] = jnp.where(valid, 1.0, 0.0).astype(jnp.bfloat16)


def first_kernel(q_ref, meta_ref, kv_ref, acc_ref, m_ref, mask_ref, ones_ref, *, cached, tokens):
    width = cached + tokens

    @pl.when(pl.program_id(0) == 0)
    def _():
        fill_ones(meta_ref, ones_ref, 0, 1, cached)
        own = jnp.broadcast_to(meta_ref[0:1, :], (tokens, tokens)).T
        for slot in range(len(ORDER)):
            seen = meta_ref[slot:slot + 1, :] <= own
            mask_ref[slot] = jnp.where(seen, 1.0, 0.0).astype(jnp.bfloat16)

    scale = LOG2E * HD ** -0.5
    q = rows_of(q_ref)
    tiles = [(kv_ref, 0, 0, t) for t in range(width // HD)]
    scores = jnp.dot(q, keys_at(tiles), preferred_element_type=jnp.float32) * scale
    lane = lax.broadcasted_iota(jnp.int32, (1, cached), 1)
    length = jnp.concatenate([meta_ref[len(ORDER):len(ORDER) + 1, :]] * (cached // HD), 1)
    bias = jnp.where(lane < length, 0.0, NEG)
    shown = jnp.concatenate([mask_ref[0].astype(jnp.float32)] * HG, 0) > 0.5
    scores = jnp.concatenate([scores[:, :cached] + bias, jnp.where(shown, scores[:, cached:], NEG)], 1)
    peak = jnp.max(scores, 1, keepdims=True)
    weights = jnp.exp2(scores - peak).astype(jnp.bfloat16)
    values = values_at(tiles, ones_ref, cached, tokens)
    acc_ref[...] = jnp.dot(weights, values, preferred_element_type=jnp.float32)
    for i in range(HG):
        m_ref[0, :, i:i + 1] = peak[i * tokens:(i + 1) * tokens, :]


def add_blocks(q_ref, m_ref, mask_ref, acc, kv_refs, ones_ref, first, cached, tokens):
    width = cached + tokens
    scale = LOG2E * HD ** -0.5
    full = cached // HD
    q = rows_of(q_ref)
    peak = jnp.concatenate([m_ref[0, :, i:i + 1] for i in range(HG)], 0)
    blocks = [(ref, base, b) for b, (ref, base) in enumerate(blocks_of(kv_refs, width))]
    for p in range(0, len(blocks), 2):
        pair = blocks[p:p + 2]
        tiles = [block + (t,) for block in pair for t in range(full)]
        tiles += [block + (t,) for block in pair for t in range(full, width // HD)]
        scores = jnp.dot(q, keys_at(tiles), preferred_element_type=jnp.float32)
        weights = jnp.exp2(scores * scale - peak).astype(jnp.bfloat16)
        at = len(pair) * cached
        parts = [weights[:, :at]]
        for i, (_, _, b) in enumerate(pair):
            seen = jnp.concatenate([mask_ref[first + b]] * HG, 0)
            parts.append(weights[:, at + i * tokens:at + (i + 1) * tokens] * seen)
        values = values_at(tiles, ones_ref, cached, tokens)
        acc = acc + jnp.dot(jnp.concatenate(parts, 1), values, preferred_element_type=jnp.float32)
    return acc


def middle_kernel(meta_ref, q_ref, m_ref, mask_ref, acc_in, *refs, first, count, cached, tokens):
    kv_refs, (acc_out, ones_ref) = refs[:-2], refs[-2:]

    @pl.when(pl.program_id(0) == 0)
    def _():
        fill_ones(meta_ref, ones_ref, first, count, cached)

    acc_out[...] = add_blocks(q_ref, m_ref, mask_ref, acc_in[...], kv_refs, ones_ref, first, cached, tokens)


def safe_rows(q_ref, mask_ref, acc_ref, peak_ref, everything, all_ref, sem, meta_ref, cached, tokens):
    width = cached + tokens
    scale = LOG2E * HD ** -0.5
    for slot, (ref, base) in enumerate(blocks_of(everything, width)):
        copy = pltpu.make_async_copy(ref.at[pl.ds(base, 2 * width)], all_ref.at[slot], sem)
        copy.start()
        copy.wait()
    q = rows_of(q_ref)
    peak_ref[...] = jnp.full(peak_ref.shape, NEG, jnp.float32)
    acc_ref[...] = jnp.zeros(acc_ref.shape, jnp.float32)

    def step(b, carry):
        keys = jnp.concatenate([all_ref[b, t * HD:(t + 1) * HD, :] for t in range(width // HD)], 1)
        scores = jnp.dot(q, keys, preferred_element_type=jnp.float32) * scale
        lane = lax.broadcasted_iota(jnp.int32, (tokens, cached), 1)
        length = jnp.concatenate([meta_ref[pl.ds(len(ORDER) + b, 1), :]] * (cached // HD), 1)
        filled = jnp.where(lane < length, 1.0, 0.0)
        seen = mask_ref[b].astype(jnp.float32)
        shown = jnp.concatenate([jnp.concatenate([filled, seen], 1)] * HG, 0) > 0.5
        scores = jnp.where(shown, scores, NEG)
        old = peak_ref[...]
        new = jnp.maximum(old, jnp.max(scores, 1, keepdims=True))
        weights = jnp.where(shown, jnp.exp2(scores - new[:, :1]), 0.0).astype(jnp.bfloat16)
        values = jnp.concatenate([all_ref[b, width:, :], jnp.ones((width, HD), jnp.bfloat16)], 1)
        factor = jnp.exp2(old - new)
        acc_ref[...] = acc_ref[...] * factor[:, :1] + jnp.dot(weights, values, preferred_element_type=jnp.float32)
        peak_ref[...] = new
        return carry

    lax.fori_loop(0, len(ORDER), step, 0)


def last_kernel(meta_ref, q_ref, m_ref, mask_ref, acc_in, *refs, first, count, parts, others, cached, tokens):
    kv_refs, others_refs = refs[:parts], refs[parts:parts + others]
    out_ref, ones_ref, acc_ref, peak_ref, all_ref, sem = refs[parts + others:]

    @pl.when(pl.program_id(0) == 0)
    def _():
        fill_ones(meta_ref, ones_ref, first, count, cached)

    def finish(acc):
        result = (acc[:, :HD] / acc[:, HD:]).astype(jnp.bfloat16)
        for i in range(HG):
            out_ref[:, i * HD:(i + 1) * HD] = result[i * tokens:(i + 1) * tokens, :]

    acc = add_blocks(q_ref, m_ref, mask_ref, acc_in[...], kv_refs, ones_ref, first, cached, tokens)
    finish(acc)
    bad = jnp.max(jnp.where(acc[:, HD:] < LIMIT, 0.0, 1.0)) > 0.5

    @pl.when(bad)
    def _():
        safe_rows(q_ref, mask_ref, acc_ref, peak_ref, others_refs, all_ref, sem, meta_ref, cached, tokens)
        finish(acc_ref[...])


def shards(queries, new_keys, new_values, cache_keys, cache_values, cache_lens, new_pos):
    tokens, cached = new_keys.shape[0], cache_keys.shape[0]
    width = cached + tokens
    groups = queries.shape[1] // (HG * HD)
    rows = HG * tokens
    positions = new_pos.reshape(-1, tokens)

    whole = pl.BlockSpec(memory_space=pltpu.VMEM)
    head_block = pl.BlockSpec((tokens, HG * HD), lambda g: (0, g))
    acc_block = pl.BlockSpec((rows, 2 * HD), lambda g: (g, 0))
    peak_block = pl.BlockSpec((1, tokens, HD), lambda g: (g, 0, 0))
    acc_shape = jax.ShapeDtypeStruct((groups * rows, 2 * HD), jnp.float32)
    peak_shape = jax.ShapeDtypeStruct((groups, tokens, HD), jnp.float32)
    mask_shape = jax.ShapeDtypeStruct((len(ORDER), tokens, tokens), jnp.bfloat16)
    params = pltpu.CompilerParams(vmem_limit_bytes=VMEM)
    cost = pl.CostEstimate(flops=1, bytes_accessed=1, transcendentals=0)

    def ones(blocks):
        return pltpu.VMEM((blocks, cached, HD), jnp.bfloat16)

    def pack():
        return pl.pallas_call(
            pack_kernel,
            in_specs=[pl.BlockSpec(memory_space=pltpu.HBM)] * 7,
            out_specs=[whole] * 3,
            out_shape=[
                pltpu.VMEM((2 * width, HD), jnp.bfloat16),
                pltpu.VMEM(queries.shape, jnp.bfloat16),
                pltpu.VMEM((2 * len(ORDER), tokens), jnp.int32),
            ],
            scratch_shapes=[
                pltpu.VMEM((width, HD), jnp.bfloat16),
                pltpu.VMEM((cached, HD), jnp.bfloat16),
                pltpu.VMEM(positions.shape, jnp.int32),
                pltpu.SMEM(cache_lens.shape, jnp.int32),
                pltpu.SemaphoreType.DMA((7,)),
            ],
            compiler_params=params,
            cost_estimate=cost,
        )(*[
            pltpu.with_memory_space_constraint(part, pltpu.HBM)
            for part in (cache_lens, cache_keys, new_keys, cache_values, new_values, queries, positions)
        ])

    def begin(own):
        return pl.pallas_call(
            functools.partial(first_kernel, cached=cached, tokens=tokens),
            grid=(groups,),
            in_specs=[head_block, whole, whole],
            out_specs=[acc_block, peak_block, whole],
            out_shape=[acc_shape, peak_shape, mask_shape],
            scratch_shapes=[ones(1)],
            compiler_params=params,
            cost_estimate=cost,
        )(query, meta, own)

    def add(acc, peak, mask, parts, first, count):
        return pl.pallas_call(
            functools.partial(middle_kernel, first=first, count=count, cached=cached, tokens=tokens),
            grid=(groups,),
            in_specs=[whole, head_block, peak_block, whole, acc_block] + [whole] * len(parts),
            out_specs=acc_block,
            out_shape=acc_shape,
            input_output_aliases={4: 0},
            scratch_shapes=[ones(count)],
            compiler_params=params,
            cost_estimate=cost,
        )(meta, query, peak, mask, acc, *parts)

    def end(acc, peak, mask, parts, first, count, everything):
        return pl.pallas_call(
            functools.partial(last_kernel, first=first, count=count, parts=len(parts), others=len(everything),
                              cached=cached, tokens=tokens),
            grid=(groups,),
            in_specs=[whole, head_block, peak_block, whole, acc_block] + [whole] * (len(parts) + len(everything)),
            out_specs=head_block,
            out_shape=jax.ShapeDtypeStruct(queries.shape, jnp.bfloat16),
            scratch_shapes=[
                ones(count),
                pltpu.VMEM((rows, 2 * HD), jnp.float32),
                pltpu.VMEM((rows, HD), jnp.float32),
                pltpu.VMEM((len(ORDER), 2 * width, HD), jnp.bfloat16),
                pltpu.SemaphoreType.DMA,
            ],
            compiler_params=params,
            cost_estimate=cost,
        )(meta, query, peak, mask, acc, *parts, *everything)

    tie = lax.optimization_barrier
    own, query, meta = pack()
    up, down = from_offset(own, -1, 0), from_offset(own, 1, 0)
    left, right = from_offset(own, 0, -1), from_offset(own, 0, 1)
    over_x = from_offset(own, 0, 2)
    acc, peak, mask = begin(own)

    acc, up, down, own_later = tie((acc, up, down, own))
    over_y = from_offset(own_later, 2, 0)
    acc = add(acc, peak, mask, [up, down], 1, 2)

    acc, up, down, left, right, over_x, over_y = tie((acc, up, down, left, right, over_x, over_y))
    column = jnp.concatenate([up, down], 0)
    diag_left, diag_right = from_offset(column, 0, -1), from_offset(column, 0, 1)
    far_up, far_down = from_offset(over_x, -1, 0), from_offset(over_x, 1, 0)
    acc = add(acc, peak, mask, [left, right, over_x, over_y], 3, 4)

    acc, far_up, far_down, over_x_later = tie((acc, far_up, far_down, over_x))
    opposite = from_offset(over_x_later, 2, 0)
    acc = add(acc, peak, mask, [far_up, far_down], 7, 2)

    acc, diag_left, diag_right, over_y_later = tie((acc, diag_left, diag_right, over_y))
    far_left, far_right = from_offset(over_y_later, 0, -1), from_offset(over_y_later, 0, 1)
    acc = add(acc, peak, mask, [diag_left, diag_right], 9, 4)

    last = [opposite, far_left, far_right]
    acc, *last = tie((acc, *last))
    everything = [own, up, down, left, right, over_x, over_y, far_up, far_down, diag_left, diag_right]
    return end(acc, peak, mask, last, 13, 3, everything + last)


def solution(mesh):
    both = P(("batch", "ctx"), "head")
    placed = (both, both, both, both, both, P("batch"), P("batch"))
    return jax.shard_map(shards, mesh=mesh, in_specs=placed, out_specs=both, check_vma=False)
```
